32 devices in a mesh: shot: 16 (over z, y, x), slab: 2 (over core).
Axes of the slice: x: 2, y: 2, z: 4, core: 2. Of those that a mesh axis runs over, the one named last changes fastest.
Arguments:
- velocity: float32 [16, 32, 32, 128], P('shot', None, 'slab'), may hold values from 0.15 to 0.45
- fwd_field: float32 [16, 64, 32, 256], P('shot', None, 'slab'), may hold values from -4 to 4
- adj_field: float32 [16, 64, 32, 256], P('shot', None, 'slab'), may hold values from -4 to 4
- aperture_anchor: int32 [16, 2], P('shot'), may hold values from 0 to 2, as said below
- source_cell: int32 [16, 16], P('shot'), may hold values from 0 to 524287
- wavelet: float32 [16, 2, 16], P('shot'), may hold values from -6 to 6
- shot_count: int32 [16], P('shot'), may hold values from 1 to 16
- receiver_cell: int32 [16, 1024], P('shot'), may hold values from 0 to 524287
- residual: float32 [16, 2, 1024], P('shot'), may hold values from -6 to 6
Outputs:
- gradient: float32 [16, 32, 32, 128], P('shot', None, 'slab')
The draws below stay inside these ranges and needn't reach their ends.
Inputs may be any that keep to these rules, and one draw needn't show every extreme that they name: `aperture_anchor`: entry g, 0 is g // 4 or one less and entry g, 1 is g % 4 or one less, each clipped so that the 2 x 2 tiles of the aperture lie in the model.
All inputs are finite; a program needn't handle non-finite values.
Results may differ from the reference program's by a relative error of at most 0.0003.
Values sent between devices are 32-bit elements; how exact they have to be, the bound alone decides.
A program may use at most 64 MiB of HBM per device.

```python
import jax
import jax.numpy as jnp
from jax import lax

XT = 32
YT = 128
TILES_Y = 4
SHOTS = 16
RECV = 1024
STEPS = 2
GROUPS = 16
TILES = 16
AX = 64
AY = 256
NZ = 32


def draw_aperture_anchor(key, part):
    first_key, second_key = jax.random.split(jax.random.fold_in(key, 17))
    groups = jnp.arange(GROUPS, dtype=jnp.int32)
    tiles_x = GROUPS // TILES_Y
    step_row = jax.random.randint(first_key, (GROUPS,), -1, 1)
    step_col = jax.random.randint(second_key, (GROUPS,), -1, 1)
    anchor_row = jnp.clip(groups // TILES_Y + step_row, 0, tiles_x - 2)
    anchor_col = jnp.clip(groups % TILES_Y + step_col, 0, TILES_Y - 2)
    return jnp.stack([anchor_row, anchor_col], axis=1).astype(jnp.int32)


def touch_ends(result, own_key, smallest, high):
    place = [jax.random.randint(jax.random.fold_in(own_key, axis), (), 0, length) for axis, length in enumerate(result.shape)]
    widest = result.shape.index(max(result.shape))
    next_to = place[:widest] + [(place[widest] + 1) % result.shape[widest]] + place[widest + 1:]
    return result.at[tuple(place)].set(smallest).at[tuple(next_to)].set(high)


def shard_levels(key, dims, shards, smallest, largest):
    def one(axis_at, parts):
        steps = jax.random.uniform(jax.random.fold_in(jax.random.fold_in(key, 6), axis_at), (parts,), jnp.float32, smallest / len(shards), largest / len(shards))
        return jnp.repeat(jnp.exp(steps), dims[axis_at] // parts).reshape((-1,) + (1,) * (len(dims) - axis_at - 1))

    loudness = one(*shards[0])
    for cut in shards[1:]:
        loudness = loudness * one(*cut)
    return loudness


def normal_values(own_key, shape, spread, reach, cuts=(), held_as=jnp.bfloat16):
    loudness = shard_levels(own_key, shape, cuts, -0.22, 0.18) if cuts else 1.0
    result = jax.random.normal(own_key, shape, jnp.float32) * spread * loudness
    return jnp.minimum(jnp.maximum(result, -reach), reach).astype(held_as)


def setup_inputs(seed: int = 0) -> dict:
    arg_keys = jax.random.split(jax.random.key(seed), 10)
    velocity = jnp.clip(0.15 + 0.29999998 * jax.random.uniform(arg_keys[0], (TILES, XT, NZ, YT), jnp.float32) ** shard_levels(arg_keys[0], (TILES, XT, NZ, YT), ((0, 16), (2, 2)), -0.2, 0.2), 0.15, 0.45)
    fwd_field = normal_values(arg_keys[1], (GROUPS, AX, NZ, AY), 0.5, 4.0, ((0, 16), (2, 2)), jnp.float32)
    adj_field = normal_values(arg_keys[2], (GROUPS, AX, NZ, AY), 0.5, 4.0, ((0, 16), (2, 2)), jnp.float32)
    aperture_anchor = draw_aperture_anchor(jax.random.fold_in(arg_keys[9], 71), 0)
    source_cell = touch_ends(jax.random.randint(arg_keys[4], (GROUPS, SHOTS), 0, AX * NZ * AY), jax.random.fold_in(arg_keys[4], 1), 0, (AX * NZ * AY) - 1).astype(jnp.int32)
    wavelet = normal_values(arg_keys[5], (GROUPS, STEPS, SHOTS), 1.0, 6.0, ((0, 16),), jnp.float32)
    shot_count = touch_ends(jax.random.randint(arg_keys[6], (GROUPS,), 1, SHOTS + 1), jax.random.fold_in(arg_keys[6], 1), 1, SHOTS).astype(jnp.int32)
    receiver_cell = touch_ends(jax.random.randint(arg_keys[7], (GROUPS, RECV), 0, AX * NZ * AY), jax.random.fold_in(arg_keys[7], 1), 0, (AX * NZ * AY) - 1).astype(jnp.int32)
    residual = normal_values(arg_keys[8], (GROUPS, STEPS, RECV), 1.0, 6.0, ((0, 16),), jnp.float32)
    return dict(velocity=velocity, fwd_field=fwd_field, adj_field=adj_field, aperture_anchor=aperture_anchor, source_cell=source_cell, wavelet=wavelet, shot_count=shot_count, receiver_cell=receiver_cell, residual=residual)


CENTRE = -205.0 / 72.0
STENCIL = (1.6, -0.2, 8.0 / 315.0, -1.0 / 560.0)


def laplace(padded_z):
    inner_depth = padded_z.shape[1] - 8
    padded = jnp.pad(padded_z, ((4, 4), (0, 0), (4, 4)))
    along_x = padded_z.shape[0]
    along_y = padded_z.shape[2]

    def window(shift_x, shift_z, shift_y):
        return padded[4 + shift_x:4 + shift_x + along_x, 4 + shift_z:4 + shift_z + inner_depth, 4 + shift_y:4 + shift_y + along_y]

    summed = (3.0 * CENTRE) * window(0, 0, 0)
    for distance in range(1, 5):
        paired = window(distance, 0, 0) + window(-distance, 0, 0)
        paired = paired + window(0, distance, 0) + window(0, -distance, 0)
        paired = paired + window(0, 0, distance) + window(0, 0, -distance)
        summed = summed + STENCIL[distance - 1] * paired
    return summed


def inject(field, positions, amounts):
    return field.reshape(-1).at[positions].add(amounts).reshape(field.shape)


def advance(initial, coefficient, positions, first_amounts, second_amounts):
    first_change = inject(coefficient * laplace(jnp.pad(initial, ((0, 0), (4, 4), (0, 0)))), positions, first_amounts)
    middle = initial + first_change
    second_change = inject(coefficient * laplace(jnp.pad(middle, ((0, 0), (4, 4), (0, 0)))), positions, second_amounts)
    return first_change, second_change


def reference(velocity, fwd_field, adj_field, aperture_anchor, source_cell, wavelet, shot_count, receiver_cell, residual):
    row_step = jnp.array([0, 0, 1, 1], dtype=jnp.int32)
    col_step = jnp.array([0, 1, 0, 1], dtype=jnp.int32)

    def one_group(summed, group_index):
        anchor_row = aperture_anchor[group_index, 0]
        anchor_col = aperture_anchor[group_index, 1]
        tile_ids = ((anchor_row + row_step) * TILES_Y + anchor_col + col_step).astype(jnp.int32)
        tiles = velocity[tile_ids].reshape(2, 2, XT, NZ, YT)
        speeds = tiles.transpose(0, 2, 3, 1, 4).reshape(2 * XT, NZ, 2 * YT)
        coefficient = speeds * speeds
        active = (jnp.arange(SHOTS, dtype=jnp.int32) < shot_count[group_index]).astype(jnp.float32)
        first_change, second_change = advance(fwd_field[group_index], coefficient, source_cell[group_index],
                                              wavelet[group_index, 0] * active, wavelet[group_index, 1] * active)
        start_adjoint = adj_field[group_index]
        back_first, back_second = advance(start_adjoint, coefficient, receiver_cell[group_index],
                                          residual[group_index, 1], residual[group_index, 0])
        later = start_adjoint + back_first
        earlier = 2.0 * later - start_adjoint + back_second
        imaged = earlier * first_change + later * second_change
        pieces = imaged.reshape(2, XT, NZ, 2, YT).transpose(0, 3, 1, 2, 4).reshape(4, XT, NZ, YT)
        return summed.at[tile_ids].add(pieces), None

    summed, unused = lax.scan(one_group, jnp.zeros(velocity.shape, jnp.float32), jnp.arange(GROUPS, dtype=jnp.int32))
    return 2.0 * velocity * summed
```

```python
import functools

import jax
import jax.numpy as jnp
import ml_dtypes
import numpy as np
from jax import lax
from jax.experimental import pallas as pl
from jax.experimental.pallas import tpu as pltpu
from jax.sharding import PartitionSpec as P

TILES_Y = 4
CENTRE = -205.0 / 72.0
STENCIL = (1.6, -0.2, 8.0 / 315.0, -1.0 / 560.0)
XB = 8
HALO = 8
MESH = pl.DeviceIdType.MESH
F32 = jnp.float32
BF16 = jnp.bfloat16


def split_matrix(values):
    high = values.astype(np.float32).astype(ml_dtypes.bfloat16)
    low = (values - high.astype(np.float64)).astype(np.float32).astype(ml_dtypes.bfloat16)
    return np.stack([high, low])


def stencil_matrices(depth, plane):
    weight = {0: 0.0}
    for distance in range(1, 5):
        weight[distance] = weight[-distance] = STENCIL[distance - 1]
    left = np.zeros((XB, depth, XB + 8, depth))
    beside = np.zeros((XB, depth, XB, depth))
    for x in range(XB):
        for z in range(depth):
            left[x, z, x + 4, z] += 3.0 * CENTRE
            for step in range(-4, 5):
                if step == 0:
                    continue
                left[x, z, x + 4 + step, z] += weight[step]
                if 0 <= z + step < depth:
                    left[x, z, x + 4, z + step] += weight[step]
                elif z + step < 0:
                    beside[x, z, x, z + step + depth] += weight[step]
                else:
                    beside[x, z, x, z + step - depth] += weight[step]
    right = np.zeros((plane, plane))
    for step in range(-4, 5):
        if step:
            right += weight[step] * np.eye(plane, k=step)
    rows = XB * depth
    return (
        split_matrix(left.reshape(rows, (XB + 8) * depth)),
        split_matrix(beside.reshape(rows, rows)),
        split_matrix(right),
    )


def dot(a, b):
    return jnp.dot(a, b, preferred_element_type=F32)


def dot3(a, b):
    return dot(a[0], b[0]) + dot(a[1], b[0]) + dot(a[0], b[1])


def kernel(
    shots,
    slabs,
    vel,
    fwd,
    adj,
    anchor,
    source,
    wavelet,
    count,
    receiver,
    residual,
    left_m,
    beside_m,
    right_m,
    out,
    field_h,
    field_l,
    halo,
    halo_h,
    halo_l,
    lap,
    inj,
    hot,
    flag_own,
    flag_up,
    flag_down,
    side,
    straight,
    picked,
    forward,
    moved,
    send_row,
    got_row,
    send_col,
    got_col,
    own_sum,
    slab_send,
    slab_recv,
    flag_send,
    flag_recv,
    side_send,
    side_recv,
    straight_send,
    straight_recv,
    picked_send,
    picked_recv,
    row_send,
    row_recv,
    col_send,
    col_recv,
):
    tile_x, depth, tile_y = vel.shape[1:]
    along_x, plane = fwd.shape[1], fwd.shape[3]
    blocks = along_x // XB
    chunks = tile_x // XB
    rows = XB * depth
    me = lax.axis_index("shot")
    layer = lax.axis_index("slab")
    home_row = me // TILES_Y
    home_col = me % TILES_Y
    has = {
        "left": home_col > 0,
        "right": home_col < TILES_Y - 1,
        "up": home_row > 0,
        "down": home_row < shots // TILES_Y - 1,
        "above": layer > 0,
        "below": layer < slabs - 1,
    }
    where = {
        "left": {"shot": me - 1},
        "right": {"shot": me + 1},
        "up": {"shot": me - TILES_Y},
        "down": {"shot": me + TILES_Y},
        "above": {"slab": layer - 1},
        "below": {"slab": layer + 1},
    }
    opposite = {
        "left": "right",
        "right": "left",
        "up": "down",
        "down": "up",
        "above": "below",
        "below": "above",
    }

    def copy_to(side_name, src, dst, send_sem, recv_sem):
        return pltpu.make_async_remote_copy(
            src_ref=src,
            dst_ref=dst,
            send_sem=send_sem,
            recv_sem=recv_sem,
            device_id=where[side_name],
            device_id_type=MESH,
        )

    def start(side_name, *parts):
        @pl.when(has[side_name])
        def _():
            copy_to(side_name, *parts).start()

    def arrived(side_name, *parts):
        source_side = opposite[side_name]

        @pl.when(has[source_side])
        def _():
            copy_to(source_side, *parts).wait_recv()

    def sent(side_name, *parts):
        @pl.when(has[side_name])
        def _():
            copy_to(side_name, *parts).wait_send()

    row_up = (home_row - anchor[0, 0]).astype(F32)
    col_left = (home_col - anchor[0, 1]).astype(F32)
    flag_own[...] = jnp.full(flag_own.shape, col_left, F32)

    for name in has:

        @pl.when(has[name])
        def _(name=name):
            pl.semaphore_signal(
                pltpu.get_barrier_semaphore(), inc=1, device_id=where[name], device_id_type=MESH
            )

    @pl.when(jnp.logical_not(has["above"]))
    def _():
        halo[:, :, HALO:, :] = jnp.zeros((4, along_x, HALO, plane), F32)

    @pl.when(jnp.logical_not(has["below"]))
    def _():
        halo[:, :, :HALO, :] = jnp.zeros((4, along_x, HALO, plane), F32)

    for index, name in enumerate(("up", "down")):

        @pl.when(jnp.logical_not(has[name]))
        def _(index=index):
            got_row[index] = jnp.zeros(got_row.shape[1:], F32)

    for index, name in enumerate(("left", "right")):

        @pl.when(jnp.logical_not(has[name]))
        def _(index=index):
            got_col[index] = jnp.zeros(got_col.shape[1:], F32)

    edge = jnp.zeros((2, 4, depth, plane), BF16)
    field_h[:, :4] = edge
    field_l[:, :4] = edge
    field_h[:, along_x + 4 :] = edge
    field_l[:, along_x + 4 :] = edge

    total = sum(has[name].astype(jnp.int32) for name in has)
    pl.semaphore_wait(pltpu.get_barrier_semaphore(), total)

    def slab_copy(name, index, src):
        layers = slice(0, HALO) if name == "above" else slice(depth - HALO, depth)
        way = 0 if name == "above" else 1
        return (
            name,
            src.at[:, layers, :],
            halo.at[index, :, layers, :],
            slab_send.at[index, way],
            slab_recv.at[index, way],
        )

    def flag_copy(name):
        dst = flag_down if name == "up" else flag_up
        way = 0 if name == "up" else 1
        return (name, flag_own, dst, flag_send.at[way], flag_recv.at[way])

    def chunk_of(k):
        return pl.ds(k * XB, XB)

    def side_copy(name, k):
        way = 0 if name == "right" else 1
        return (
            name,
            vel.at[0, chunk_of(k)],
            side.at[way, chunk_of(k)],
            side_send.at[way, k],
            side_recv.at[way, k],
        )

    def straight_copy(name):
        way = 0 if name == "down" else 1
        return (name, vel.at[0], straight.at[way], straight_send.at[way], straight_recv.at[way])

    def picked_copy(name, k):
        way = 0 if name == "down" else 1
        return (
            name,
            forward.at[way, chunk_of(k)],
            picked.at[way, chunk_of(k)],
            picked_send.at[way, k],
            picked_recv.at[way, k],
        )

    def row_copy(name, part, k):
        way = 0 if name == "down" else 1
        return (
            name,
            send_row.at[way, part, chunk_of(k)],
            got_row.at[way, part, chunk_of(k)],
            row_send.at[way, part, k],
            row_recv.at[way, part, k],
        )

    def col_copy(name, k):
        way = 0 if name == "right" else 1
        return (
            name,
            send_col.at[way, chunk_of(k)],
            got_col.at[way, chunk_of(k)],
            col_send.at[way, k],
            col_recv.at[way, k],
        )

    for name in ("up", "down"):
        start(*flag_copy(name))
    for k in range(chunks):
        for name in ("left", "right"):
            start(*side_copy(name, k))
        if k == 0:
            for index, src in enumerate((fwd.at[0], adj.at[0])):
                for name in ("above", "below"):
                    start(*slab_copy(name, index, src))
            for name in ("up", "down"):
                start(*straight_copy(name))

    def mask_of(flag_value, shape):
        return jnp.broadcast_to(flag_value, shape) > 0.5

    def split_to(high_ref, low_ref, index, at, value):
        high = value.astype(BF16)
        high_ref[index, at] = high
        low_ref[index, at] = (value - high.astype(F32)).astype(BF16)

    def split_field(index, src):
        @pl.loop(0, blocks)
        def _(b):
            split_to(field_h, field_l, index, pl.ds(b * XB + 4, XB), src[0, pl.ds(b * XB, XB)])

    def split_halo(index):
        @pl.loop(0, blocks)
        def _(b):
            at = pl.ds(b * XB, XB)
            split_to(halo_h, halo_l, index % 2, at, halo[index, at])

    def laplace(index, b):
        wide = pl.ds(b * XB, XB + 8)
        shape = ((XB + 8) * depth, plane)
        block = (field_h[index, wide].reshape(shape), field_l[index, wide].reshape(shape))
        at = pl.ds(b * XB, XB)
        near = (halo_h[index, at].reshape(rows, plane), halo_l[index, at].reshape(rows, plane))
        inner = tuple(part[4 * depth : 4 * depth + rows] for part in block)
        summed = dot3((left_m[0], left_m[1]), block)
        summed = summed + dot3((beside_m[0], beside_m[1]), near)
        summed = summed + dot3(inner, (right_m[0], right_m[1]))
        return summed.reshape(XB, depth, plane)

    def first_laplace(index):
        @pl.loop(0, blocks)
        def _(b):
            lap[index, pl.ds(b * XB, XB)] = laplace(index, b)

    first_layer = layer * depth
    total_depth = depth * slabs

    def whole_part(value, divisor):
        return ((value.astype(F32) + 0.5) * (1.0 / divisor)).astype(jnp.int32)

    def injections(index, positions, amounts):
        lanes = positions.shape[1]
        line = whole_part(positions, plane)
        cell_y = positions - line * plane
        cell_x = whole_part(line, total_depth)
        cell_z = line - cell_x * total_depth - first_layer
        inside = (cell_z >= 0) & (cell_z < depth)
        row_index = jnp.where(inside, cell_x * depth + cell_z, -1)
        col_hot = lax.broadcasted_iota(jnp.int32, (plane, lanes), 0) == cell_y
        for step in range(2):
            amount = amounts[step]
            high = amount.astype(BF16).astype(F32)
            for part, value in enumerate((high, amount - high)):
                at = (2 * step + part) * plane
                hot[at : at + plane, :lanes] = jnp.where(col_hot, value, 0.0).astype(BF16)
        tall = 2 * rows

        @pl.loop(0, along_x * depth // tall)
        def _(b):
            ids = lax.broadcasted_iota(jnp.int32, (tall, lanes), 0) + b * tall
            rows_hot = jnp.where(ids == row_index, 1.0, 0.0).astype(BF16)
            for step in range(2):
                cols = hot[2 * step * plane : 2 * (step + 1) * plane, :lanes]
                both = lax.dot_general(
                    rows_hot, cols, (((1,), (1,)), ((), ())), preferred_element_type=F32
                )
                added = both[:, :plane] + both[:, plane:]
                inj[2 * index + step, pl.ds(b * 2 * XB, 2 * XB)] = added.reshape(
                    2 * XB, depth, plane
                )

    def pass_on(k):
        for name in ("left", "right"):
            arrived(*side_copy(name, k))
        if k == 0:
            for name in ("up", "down"):
                arrived(*flag_copy(name))
        for way, flag in ((1, flag_up), (0, flag_down)):
            picks = mask_of(flag[...][None], (XB, depth, tile_y))
            forward[way, chunk_of(k)] = jnp.where(picks, side[0, chunk_of(k)], side[1, chunk_of(k)])
        for name in ("up", "down"):
            start(*picked_copy(name, k))

    split_field(0, fwd)
    split_field(1, adj)
    lane = lax.broadcasted_iota(jnp.int32, source.shape, 1)
    active = jnp.where(lane < count[0], 1.0, 0.0)
    injections(0, source[...], (wavelet[0, 0:1] * active, wavelet[0, 1:2] * active))
    pass_on(0)
    for index in range(2):
        for name in ("above", "below"):
            arrived(*slab_copy(name, index, (fwd, adj)[index].at[0]))
        split_halo(index)
    first_laplace(0)
    pass_on(1)
    injections(1, receiver[...], (residual[0, 1:2], residual[0, 0:1]))
    pass_on(2)
    first_laplace(1)
    pass_on(3)
    for k in range(4, chunks):
        pass_on(k)
    for name in ("up", "down"):
        arrived(*straight_copy(name))
        for k in range(chunks):
            arrived(*picked_copy(name, k))

    shape = (XB, depth, tile_y)
    is_left = mask_of(jnp.full(shape, col_left, F32), shape)
    is_up = mask_of(jnp.full(shape, row_up, F32), shape)

    def coefficient(part_row, k):
        at = chunk_of(k)
        own_same, own_other = vel[0, at], jnp.where(is_left, side[0, at], side[1, at])
        same, other = straight[part_row, at], picked[part_row, at]
        own_here = is_up if part_row == 1 else jnp.logical_not(is_up)
        same = jnp.where(own_here, own_same, same)
        other = jnp.where(own_here, own_other, other)
        speeds = jnp.concatenate(
            [jnp.where(is_left, other, same), jnp.where(is_left, same, other)], axis=2
        )
        return speeds * speeds

    for part_row in range(2):

        @pl.loop(0, chunks)
        def _(k):
            squares = coefficient(part_row, k)
            x = part_row * tile_x + k * XB
            at = pl.ds(x, XB)
            for index, src in enumerate((fwd, adj)):
                change = squares * lap[index, at] + inj[2 * index, at]
                lap[index, at] = change
                later = src[0, at] + change
                moved[index, at] = later
                split_to(field_h, field_l, index, pl.ds(x + 4, XB), later)

    for index in range(2):
        for name in ("above", "below"):
            start(*slab_copy(name, 2 + index, moved.at[index]))
    for index in range(2):
        for name in ("above", "below"):
            arrived(*slab_copy(name, 2 + index, moved.at[index]))
        split_halo(2 + index)

    def image(part_row, k):
        squares = coefficient(part_row, k)
        x = part_row * tile_x + k * XB
        b = part_row * chunks + k
        at = pl.ds(x, XB)
        second = squares * laplace(0, b) + inj[1, at]
        back = squares * laplace(1, b) + inj[3, at]
        later = moved[1, at]
        earlier = 2.0 * later - adj[0, at] + back
        whole = earlier * lap[0, at] + later * second
        low, high = whole[:, :, :tile_y], whole[:, :, tile_y:]
        return jnp.where(is_left, high, low), jnp.where(is_left, low, high)

    for k in range(chunks):
        at = chunk_of(k)
        first_same, first_other = image(0, k)
        last_same, last_other = image(1, k)
        send_row[1, 0, at] = jnp.where(is_up, first_other, 0.0)
        send_row[0, 0, at] = jnp.where(is_up, 0.0, last_other)
        send_row[1, 1, at] = jnp.where(is_up, first_same, 0.0)
        send_row[0, 1, at] = jnp.where(is_up, 0.0, last_same)
        for part in range(2):
            for name in ("up", "down"):
                start(*row_copy(name, part, k))
        own_sum[at] = jnp.where(is_up, last_same, first_same)
        own_other = jnp.where(is_up, last_other, first_other)
        send_col[1, at] = jnp.where(is_left, own_other, 0.0)
        send_col[0, at] = jnp.where(is_left, 0.0, own_other)

    for k in range(chunks):
        at = chunk_of(k)
        for name in ("up", "down"):
            arrived(*row_copy(name, 0, k))
        for way, flag in ((0, flag_up), (1, flag_down)):
            picks = mask_of(flag[...][None], shape)
            piece = got_row[way, 0, at]
            send_col[1, at] = send_col[1, at] + jnp.where(picks, piece, 0.0)
            send_col[0, at] = send_col[0, at] + jnp.where(picks, 0.0, piece)
        for name in ("left", "right"):
            start(*col_copy(name, k))
    for k in range(chunks):
        at = chunk_of(k)
        for name in ("up", "down"):
            arrived(*row_copy(name, 1, k))
        for name in ("left", "right"):
            arrived(*col_copy(name, k))
        summed = own_sum[at] + got_row[0, 1, at] + got_row[1, 1, at]
        out[0, at] = 2.0 * vel[0, at] * (summed + got_col[0, at] + got_col[1, at])

    for name in ("up", "down"):
        sent(*flag_copy(name))
        sent(*straight_copy(name))
        for k in range(chunks):
            sent(*picked_copy(name, k))
            for part in range(2):
                sent(*row_copy(name, part, k))
    for name in ("left", "right"):
        for k in range(chunks):
            sent(*side_copy(name, k))
            sent(*col_copy(name, k))
    for index in range(2):
        for name in ("above", "below"):
            sent(*slab_copy(name, index, (fwd, adj)[index].at[0]))
            sent(*slab_copy(name, 2 + index, moved.at[index]))


def body(shots, slabs, velocity, fwd_field, adj_field, anchor, source, wavelet, count, receiver, residual):
    tile_x, depth, tile_y = velocity.shape[1:]
    along_x, plane = fwd_field.shape[1], fwd_field.shape[3]
    chunks = tile_x // XB
    left_m, beside_m, right_m = (jnp.asarray(m) for m in stencil_matrices(depth, plane))
    vmem = pl.BlockSpec(memory_space=pltpu.VMEM)
    smem = pl.BlockSpec(memory_space=pltpu.SMEM)
    aperture = (along_x, depth, plane)
    tile = (tile_x, depth, tile_y)
    dma = pltpu.SemaphoreType.DMA
    lanes = receiver.shape[1]
    return pl.pallas_call(
        functools.partial(kernel, shots, slabs),
        out_shape=jax.ShapeDtypeStruct(velocity.shape, F32),
        in_specs=[vmem, vmem, vmem, smem, vmem, vmem, smem, vmem, vmem, vmem, vmem, vmem],
        out_specs=vmem,
        scratch_shapes=[
            pltpu.VMEM((2, along_x + 8, depth, plane), BF16),
            pltpu.VMEM((2, along_x + 8, depth, plane), BF16),
            pltpu.VMEM((4,) + aperture, F32),
            pltpu.VMEM((2,) + aperture, BF16),
            pltpu.VMEM((2,) + aperture, BF16),
            pltpu.VMEM((2,) + aperture, F32),
            pltpu.VMEM((4,) + aperture, F32),
            pltpu.VMEM((4 * plane, lanes), BF16),
            pltpu.VMEM((depth, tile_y), F32),
            pltpu.VMEM((depth, tile_y), F32),
            pltpu.VMEM((depth, tile_y), F32),
            pltpu.VMEM((2,) + tile, F32),
            pltpu.VMEM((2,) + tile, F32),
            pltpu.VMEM((2,) + tile, F32),
            pltpu.VMEM((2,) + tile, F32),
            pltpu.VMEM((2,) + aperture, F32),
            pltpu.VMEM((2, 2) + tile, F32),
            pltpu.VMEM((2, 2) + tile, F32),
            pltpu.VMEM((2,) + tile, F32),
            pltpu.VMEM((2,) + tile, F32),
            pltpu.VMEM(tile, F32),
            dma((4, 2)),
            dma((4, 2)),
            dma((2,)),
            dma((2,)),
            dma((2, chunks)),
            dma((2, chunks)),
            dma((2,)),
            dma((2,)),
            dma((2, chunks)),
            dma((2, chunks)),
            dma((2, 2, chunks)),
            dma((2, 2, chunks)),
            dma((2, chunks)),
            dma((2, chunks)),
        ],
        compiler_params=pltpu.CompilerParams(
            collective_id=0, has_side_effects=True, vmem_limit_bytes=48 * 1024 * 1024
        ),
    )(
        velocity, fwd_field, adj_field, anchor, source, wavelet, count, receiver, residual,
        left_m, beside_m, right_m,
    )


def solution(mesh):
    placed = (
        P("shot", None, "slab", None),
        P("shot", None, "slab", None),
        P("shot", None, "slab", None),
        P("shot", None),
        P("shot", None),
        P("shot", None, None),
        P("shot"),
        P("shot", None),
        P("shot", None, None),
    )
    return jax.shard_map(
        functools.partial(body, mesh.shape["shot"], mesh.shape["slab"]),
        mesh=mesh,
        in_specs=placed,
        out_specs=P("shot", None, "slab", None),
        check_vma=False,
    )
```

```python
import functools

import jax
import jax.numpy as jnp
import ml_dtypes
import numpy as np
from jax import lax
from jax.experimental import pallas as pl
from jax.experimental.pallas import tpu as pltpu
from jax.sharding import PartitionSpec as P

TILES_Y = 4
CENTRE = -205.0 / 72.0
STENCIL = (1.6, -0.2, 8.0 / 315.0, -1.0 / 560.0)
XB = 8
OPERANDS = 12
HALO = 8
MESH = pl.DeviceIdType.MESH
F32 = jnp.float32
BF16 = jnp.bfloat16


def split_matrix(values):
    high = values.astype(np.float32).astype(ml_dtypes.bfloat16)
    low = (values - high.astype(np.float64)).astype(np.float32).astype(ml_dtypes.bfloat16)
    return np.stack([high, low])


def stencil_matrices(depth, plane):
    weight = {0: 0.0}
    for distance in range(1, 5):
        weight[distance] = weight[-distance] = STENCIL[distance - 1]
    left = np.zeros((XB, depth, XB + 8, depth))
    beside = np.zeros((XB, depth, XB, depth))
    for x in range(XB):
        for z in range(depth):
            left[x, z, x + 4, z] += 3.0 * CENTRE
            for step in range(-4, 5):
                if step == 0:
                    continue
                left[x, z, x + 4 + step, z] += weight[step]
                if 0 <= z + step < depth:
                    left[x, z, x + 4, z + step] += weight[step]
                elif z + step < 0:
                    beside[x, z, x, z + step + depth] += weight[step]
                else:
                    beside[x, z, x, z + step - depth] += weight[step]
    right = np.zeros((plane, plane))
    for step in range(-4, 5):
        if step:
            right += weight[step] * np.eye(plane, k=step)
    rows = XB * depth
    return (
        split_matrix(left.reshape(rows, (XB + 8) * depth)),
        split_matrix(beside.reshape(rows, rows)),
        split_matrix(right),
    )


def dot(a, b):
    return jnp.dot(a, b, preferred_element_type=F32)


def dot3(a, b):
    return dot(a[0], b[0]) + dot(a[1], b[0]) + dot(a[0], b[1])


def kernel(
    shots,
    slabs,
    *refs,
):
    operands, refs = refs[:OPERANDS], refs[OPERANDS:]
    out, held, rest = refs[0], refs[1 : 1 + OPERANDS], refs[1 + OPERANDS :]
    compute(shots, slabs, operands, held, out, *rest)


def compute(
    shots,
    slabs,
    operands,
    held,
    out,
    load_sem,
    field_h,
    field_l,
    halo,
    lap,
    inj,
    hot,
    flag_own,
    flag_up,
    flag_down,
    side,
    straight,
    picked,
    forward,
    moved,
    send_row,
    got_row,
    send_col,
    got_col,
    own_sum,
    slab_send,
    slab_recv,
    moved_send,
    moved_recv,
    flag_send,
    flag_recv,
    side_send,
    side_recv,
    straight_send,
    straight_recv,
    picked_send,
    picked_recv,
    row_send,
    row_recv,
    col_send,
    col_recv,
):
    loads = [
        pltpu.make_async_copy(src, dst, load_sem.at[i])
        for i, (src, dst) in enumerate(zip(operands, held))
    ]
    vel, fwd, adj, anchor, source, wavelet, count, receiver, residual = held[:9]
    left_m, beside_m, right_m = held[9:]
    for load in loads:
        load.start()
    tile_x, depth, tile_y = vel.shape[1:]
    along_x, plane = fwd.shape[1], fwd.shape[3]
    blocks = along_x // XB
    chunks = tile_x // XB
    rows = XB * depth
    me = lax.axis_index("shot")
    layer = lax.axis_index("slab")
    home_row = me // TILES_Y
    home_col = me % TILES_Y
    has = {
        "left": home_col > 0,
        "right": home_col < TILES_Y - 1,
        "up": home_row > 0,
        "down": home_row < shots // TILES_Y - 1,
        "above": layer > 0,
        "below": layer < slabs - 1,
    }
    where = {
        "left": {"shot": me - 1},
        "right": {"shot": me + 1},
        "up": {"shot": me - TILES_Y},
        "down": {"shot": me + TILES_Y},
        "above": {"slab": layer - 1},
        "below": {"slab": layer + 1},
    }
    opposite = {
        "left": "right",
        "right": "left",
        "up": "down",
        "down": "up",
        "above": "below",
        "below": "above",
    }

    def copy_to(side_name, src, dst, send_sem, recv_sem):
        return pltpu.make_async_remote_copy(
            src_ref=src,
            dst_ref=dst,
            send_sem=send_sem,
            recv_sem=recv_sem,
            device_id=where[side_name],
            device_id_type=MESH,
        )

    def start(side_name, *parts):
        @pl.when(has[side_name])
        def _():
            copy_to(side_name, *parts).start()

    def arrived(side_name, *parts):
        source_side = opposite[side_name]

        @pl.when(has[source_side])
        def _():
            copy_to(source_side, *parts).wait_recv()

    def sent(side_name, *parts):
        @pl.when(has[side_name])
        def _():
            copy_to(side_name, *parts).wait_send()

    for name in has:

        @pl.when(has[name])
        def _(name=name):
            pl.semaphore_signal(
                pltpu.get_barrier_semaphore(), inc=1, device_id=where[name], device_id_type=MESH
            )

    @pl.when(jnp.logical_not(has["above"]))
    def _():
        halo[:, :, HALO:, :] = jnp.zeros((4, along_x, HALO, plane), F32)

    @pl.when(jnp.logical_not(has["below"]))
    def _():
        halo[:, :, :HALO, :] = jnp.zeros((4, along_x, HALO, plane), F32)

    for index, name in enumerate(("up", "down")):

        @pl.when(jnp.logical_not(has[name]))
        def _(index=index):
            got_row[index] = jnp.zeros(got_row.shape[1:], F32)

    for index, name in enumerate(("left", "right")):

        @pl.when(jnp.logical_not(has[name]))
        def _(index=index):
            got_col[index] = jnp.zeros(got_col.shape[1:], F32)

    edge = jnp.zeros((2, 4, depth, plane), BF16)
    field_h[:, :4] = edge
    field_l[:, :4] = edge
    field_h[:, along_x + 4 :] = edge
    field_l[:, along_x + 4 :] = edge

    loads[0].wait()
    loads[3].wait()
    row_up = (home_row - anchor[0, 0]).astype(F32)
    col_left = (home_col - anchor[0, 1]).astype(F32)
    flag_own[...] = jnp.full(flag_own.shape, col_left, F32)

    total = sum(has[name].astype(jnp.int32) for name in has)
    pl.semaphore_wait(pltpu.get_barrier_semaphore(), total)

    def slab_copy(name, index, src):
        layers = slice(0, HALO) if name == "above" else slice(depth - HALO, depth)
        way = 0 if name == "above" else 1
        return (
            name,
            src.at[:, layers, :],
            halo.at[index, :, layers, :],
            slab_send.at[index, way],
            slab_recv.at[index, way],
        )

    def flag_copy(name):
        dst = flag_down if name == "up" else flag_up
        way = 0 if name == "up" else 1
        return (name, flag_own, dst, flag_send.at[way], flag_recv.at[way])

    def chunk_of(k):
        return pl.ds(k * XB, XB)

    def side_copy(name, k):
        way = 0 if name == "right" else 1
        return (
            name,
            vel.at[0, chunk_of(k)],
            side.at[way, chunk_of(k)],
            side_send.at[way, k],
            side_recv.at[way, k],
        )

    def straight_copy(name):
        way = 0 if name == "down" else 1
        return (name, vel.at[0], straight.at[way], straight_send.at[way], straight_recv.at[way])

    def picked_copy(name, k):
        way = 0 if name == "down" else 1
        return (
            name,
            forward.at[way, chunk_of(k)],
            picked.at[way, chunk_of(k)],
            picked_send.at[way, k],
            picked_recv.at[way, k],
        )

    def row_copy(name, part, k):
        way = 0 if name == "down" else 1
        return (
            name,
            send_row.at[way, part, chunk_of(k)],
            got_row.at[way, part, chunk_of(k)],
            row_send.at[way, part, k],
            row_recv.at[way, part, k],
        )

    def col_copy(name, k):
        way = 0 if name == "right" else 1
        return (
            name,
            send_col.at[way, chunk_of(k)],
            got_col.at[way, chunk_of(k)],
            col_send.at[way, k],
            col_recv.at[way, k],
        )

    for name in ("up", "down"):
        start(*flag_copy(name))
    for k in range(chunks):
        for name in ("left", "right"):
            start(*side_copy(name, k))
        if k == 0:
            for load in loads[1:3]:
                load.wait()
            for index, src in enumerate((fwd.at[0], adj.at[0])):
                for name in ("above", "below"):
                    start(*slab_copy(name, index, src))
            for name in ("up", "down"):
                start(*straight_copy(name))

    def mask_of(flag_value, shape):
        return jnp.broadcast_to(flag_value, shape) > 0.5

    def split_to(high_ref, low_ref, index, at, value):
        high = value.astype(BF16)
        high_ref[index, at] = high
        low_ref[index, at] = (value - high.astype(F32)).astype(BF16)

    def split_field(index, src):
        @pl.loop(0, blocks)
        def _(b):
            split_to(field_h, field_l, index, pl.ds(b * XB + 4, XB), src[0, pl.ds(b * XB, XB)])

    def laplace(index, b, beside):
        wide = pl.ds(b * XB, XB + 8)
        shape = ((XB + 8) * depth, plane)
        block = (field_h[index, wide].reshape(shape), field_l[index, wide].reshape(shape))
        at = pl.ds(b * XB, XB)
        near = halo[beside, at].reshape(rows, plane)
        near_h = near.astype(BF16)
        near = (near_h, (near - near_h.astype(F32)).astype(BF16))
        inner = tuple(part[4 * depth : 4 * depth + rows] for part in block)
        summed = dot3((left_m[0], left_m[1]), block)
        summed = summed + dot3((beside_m[0], beside_m[1]), near)
        summed = summed + dot3(inner, (right_m[0], right_m[1]))
        return summed.reshape(XB, depth, plane)

    def first_laplace(index):
        @pl.loop(0, blocks)
        def _(b):
            lap[index, pl.ds(b * XB, XB)] = laplace(index, b, index)

    first_layer = layer * depth
    total_depth = depth * slabs

    def whole_part(value, divisor):
        return ((value.astype(F32) + 0.5) * (1.0 / divisor)).astype(jnp.int32)

    def injections(index, positions, amounts):
        lanes = positions.shape[1]
        line = whole_part(positions, plane)
        cell_y = positions - line * plane
        cell_x = whole_part(line, total_depth)
        cell_z = line - cell_x * total_depth - first_layer
        inside = (cell_z >= 0) & (cell_z < depth)
        row_index = jnp.where(inside, cell_x * depth + cell_z, -1)
        col_hot = lax.broadcasted_iota(jnp.int32, (plane, lanes), 0) == cell_y
        for step in range(2):
            amount = amounts[step]
            high = amount.astype(BF16).astype(F32)
            for part, value in enumerate((high, amount - high)):
                at = (2 * step + part) * plane
                hot[at : at + plane, :lanes] = jnp.where(col_hot, value, 0.0).astype(BF16)
        tall = 2 * rows

        @pl.loop(0, along_x * depth // tall)
        def _(b):
            ids = lax.broadcasted_iota(jnp.int32, (tall, lanes), 0) + b * tall
            rows_hot = jnp.where(ids == row_index, 1.0, 0.0).astype(BF16)
            for step in range(2):
                cols = hot[2 * step * plane : 2 * (step + 1) * plane, :lanes]
                both = lax.dot_general(
                    rows_hot, cols, (((1,), (1,)), ((), ())), preferred_element_type=F32
                )
                added = both[:, :plane] + both[:, plane:]
                inj[2 * index + step, pl.ds(b * 2 * XB, 2 * XB)] = added.reshape(
                    2 * XB, depth, plane
                )

    def pass_on(k):
        for name in ("left", "right"):
            arrived(*side_copy(name, k))
        if k == 0:
            for name in ("up", "down"):
                arrived(*flag_copy(name))
        for way, flag in ((1, flag_up), (0, flag_down)):
            picks = mask_of(flag[...][None], (XB, depth, tile_y))
            forward[way, chunk_of(k)] = jnp.where(picks, side[0, chunk_of(k)], side[1, chunk_of(k)])
        for name in ("up", "down"):
            start(*picked_copy(name, k))

    for load in loads[4:]:
        load.wait()
    split_field(0, fwd)
    split_field(1, adj)
    lane = lax.broadcasted_iota(jnp.int32, source.shape, 1)
    active = jnp.where(lane < count[0], 1.0, 0.0)
    injections(0, source[...], (wavelet[0, 0:1] * active, wavelet[0, 1:2] * active))
    pass_on(0)
    for index in range(2):
        for name in ("above", "below"):
            arrived(*slab_copy(name, index, (fwd, adj)[index].at[0]))
    first_laplace(0)
    pass_on(1)
    injections(1, receiver[...], (residual[0, 1:2], residual[0, 0:1]))
    pass_on(2)
    first_laplace(1)
    pass_on(3)
    for k in range(4, chunks):
        pass_on(k)
    for name in ("up", "down"):
        arrived(*straight_copy(name))

    shape = (XB, depth, tile_y)
    is_left = mask_of(jnp.full(shape, col_left, F32), shape)
    is_up = mask_of(jnp.full(shape, row_up, F32), shape)

    def coefficient(part_row, k):
        at = chunk_of(k)
        own_same, own_other = vel[0, at], jnp.where(is_left, side[0, at], side[1, at])
        same, other = straight[part_row, at], picked[part_row, at]
        own_here = is_up if part_row == 1 else jnp.logical_not(is_up)
        same = jnp.where(own_here, own_same, same)
        other = jnp.where(own_here, own_other, other)
        speeds = jnp.concatenate(
            [jnp.where(is_left, other, same), jnp.where(is_left, same, other)], axis=2
        )
        return speeds * speeds

    def moved_copy(name, index, b):
        layers = slice(0, HALO) if name == "above" else slice(depth - HALO, depth)
        way = 0 if name == "above" else 1
        at = pl.ds(b * XB, XB)
        return (
            name,
            moved.at[index, at, layers, :],
            halo.at[2 + index, at, layers, :],
            moved_send.at[index, way, b],
            moved_recv.at[index, way, b],
        )

    for k in range(chunks):
        for name in ("up", "down"):
            arrived(*picked_copy(name, k))
        for part_row in range(2):
            squares = coefficient(part_row, k)
            x = part_row * tile_x + k * XB
            at = pl.ds(x, XB)
            for index, src in enumerate((fwd, adj)):
                change = squares * lap[index, at] + inj[2 * index, at]
                lap[index, at] = change
                later = src[0, at] + change
                moved[index, at] = later
                split_to(field_h, field_l, index, pl.ds(x + 4, XB), later)
                for name in ("above", "below"):
                    start(*moved_copy(name, index, part_row * chunks + k))

    def image(part_row, k):
        squares = coefficient(part_row, k)
        x = part_row * tile_x + k * XB
        b = part_row * chunks + k
        at = pl.ds(x, XB)
        second = squares * laplace(0, b, 2) + inj[1, at]
        back = squares * laplace(1, b, 3) + inj[3, at]
        later = moved[1, at]
        earlier = 2.0 * later - adj[0, at] + back
        whole = earlier * lap[0, at] + later * second
        low, high = whole[:, :, :tile_y], whole[:, :, tile_y:]
        return jnp.where(is_left, high, low), jnp.where(is_left, low, high)

    def along_row(k):
        at = chunk_of(k)
        for name in ("up", "down"):
            arrived(*row_copy(name, 0, k))
        for way, flag in ((0, flag_up), (1, flag_down)):
            picks = mask_of(flag[...][None], shape)
            piece = got_row[way, 0, at]
            send_col[1, at] = send_col[1, at] + jnp.where(picks, piece, 0.0)
            send_col[0, at] = send_col[0, at] + jnp.where(picks, 0.0, piece)
        for name in ("left", "right"):
            start(*col_copy(name, k))

    for k in range(chunks):
        at = chunk_of(k)
        for part_row in range(2):
            for index in range(2):
                for name in ("above", "below"):
                    arrived(*moved_copy(name, index, part_row * chunks + k))
        first_same, first_other = image(0, k)
        last_same, last_other = image(1, k)
        send_row[1, 0, at] = jnp.where(is_up, first_other, 0.0)
        send_row[0, 0, at] = jnp.where(is_up, 0.0, last_other)
        for name in ("up", "down"):
            start(*row_copy(name, 0, k))
        send_row[1, 1, at] = jnp.where(is_up, first_same, 0.0)
        send_row[0, 1, at] = jnp.where(is_up, 0.0, last_same)
        for name in ("up", "down"):
            start(*row_copy(name, 1, k))
        own_sum[at] = jnp.where(is_up, last_same, first_same)
        own_other = jnp.where(is_up, last_other, first_other)
        send_col[1, at] = jnp.where(is_left, own_other, 0.0)
        send_col[0, at] = jnp.where(is_left, 0.0, own_other)
        if k:
            along_row(k - 1)
    along_row(chunks - 1)
    for k in range(chunks):
        at = chunk_of(k)
        for name in ("up", "down"):
            arrived(*row_copy(name, 1, k))
        for name in ("left", "right"):
            arrived(*col_copy(name, k))
        summed = own_sum[at] + got_row[0, 1, at] + got_row[1, 1, at]
        out[0, at] = 2.0 * vel[0, at] * (summed + got_col[0, at] + got_col[1, at])

    for name in ("up", "down"):
        sent(*flag_copy(name))
        sent(*straight_copy(name))
        for k in range(chunks):
            sent(*picked_copy(name, k))
            for part in range(2):
                sent(*row_copy(name, part, k))
    for name in ("left", "right"):
        for k in range(chunks):
            sent(*side_copy(name, k))
            sent(*col_copy(name, k))
    for index in range(2):
        for name in ("above", "below"):
            sent(*slab_copy(name, index, (fwd, adj)[index].at[0]))
            for b in range(blocks):
                sent(*moved_copy(name, index, b))


def body(shots, slabs, velocity, fwd_field, adj_field, anchor, source, wavelet, count, receiver, residual):
    tile_x, depth, tile_y = velocity.shape[1:]
    along_x, plane = fwd_field.shape[1], fwd_field.shape[3]
    chunks = tile_x // XB
    left_m, beside_m, right_m = (jnp.asarray(m) for m in stencil_matrices(depth, plane))
    vmem = pl.BlockSpec(memory_space=pltpu.VMEM)
    operands = (
        velocity, fwd_field, adj_field, anchor, source, wavelet, count, receiver, residual,
        left_m, beside_m, right_m,
    )
    scalars = (3, 6)
    aperture = (along_x, depth, plane)
    tile = (tile_x, depth, tile_y)
    dma = pltpu.SemaphoreType.DMA
    lanes = receiver.shape[1]
    return pl.pallas_call(
        functools.partial(kernel, shots, slabs),
        out_shape=jax.ShapeDtypeStruct(velocity.shape, F32),
        in_specs=[pl.BlockSpec(memory_space=pltpu.HBM)] * OPERANDS,
        out_specs=vmem,
        scratch_shapes=[
            (pltpu.SMEM if i in scalars else pltpu.VMEM)(operand.shape, operand.dtype)
            for i, operand in enumerate(operands)
        ]
        + [
            dma((OPERANDS,)),
            pltpu.VMEM((2, along_x + 8, depth, plane), BF16),
            pltpu.VMEM((2, along_x + 8, depth, plane), BF16),
            pltpu.VMEM((4,) + aperture, F32),
            pltpu.VMEM((2,) + aperture, F32),
            pltpu.VMEM((4,) + aperture, F32),
            pltpu.VMEM((4 * plane, lanes), BF16),
            pltpu.VMEM((depth, tile_y), F32),
            pltpu.VMEM((depth, tile_y), F32),
            pltpu.VMEM((depth, tile_y), F32),
            pltpu.VMEM((2,) + tile, F32),
            pltpu.VMEM((2,) + tile, F32),
            pltpu.VMEM((2,) + tile, F32),
            pltpu.VMEM((2,) + tile, F32),
            pltpu.VMEM((2,) + aperture, F32),
            pltpu.VMEM((2, 2) + tile, F32),
            pltpu.VMEM((2, 2) + tile, F32),
            pltpu.VMEM((2,) + tile, F32),
            pltpu.VMEM((2,) + tile, F32),
            pltpu.VMEM(tile, F32),
            dma((2, 2)),
            dma((2, 2)),
            dma((2, 2, 2 * chunks)),
            dma((2, 2, 2 * chunks)),
            dma((2,)),
            dma((2,)),
            dma((2, chunks)),
            dma((2, chunks)),
            dma((2,)),
            dma((2,)),
            dma((2, chunks)),
            dma((2, chunks)),
            dma((2, 2, chunks)),
            dma((2, 2, chunks)),
            dma((2, chunks)),
            dma((2, chunks)),
        ],
        compiler_params=pltpu.CompilerParams(
            collective_id=0, has_side_effects=True, vmem_limit_bytes=60 * 1024 * 1024
        ),
    )(*operands)


def solution(mesh):
    placed = (
        P("shot", None, "slab", None),
        P("shot", None, "slab", None),
        P("shot", None, "slab", None),
        P("shot", None),
        P("shot", None),
        P("shot", None, None),
        P("shot"),
        P("shot", None),
        P("shot", None, None),
    )
    return jax.shard_map(
        functools.partial(body, mesh.shape["shot"], mesh.shape["slab"]),
        mesh=mesh,
        in_specs=placed,
        out_specs=P("shot", None, "slab", None),
        check_vma=False,
    )
```

```python
import functools

import jax
import jax.numpy as jnp
import ml_dtypes
import numpy as np
from jax import lax
from jax.experimental import pallas as pl
from jax.experimental.pallas import tpu as pltpu
from jax.sharding import PartitionSpec as P

TILES_Y = 4
CENTRE = -205.0 / 72.0
STENCIL = (1.6, -0.2, 8.0 / 315.0, -1.0 / 560.0)
XB = 8
OPERANDS = 12
HALO = 8
MESH = pl.DeviceIdType.MESH
F32 = jnp.float32
BF16 = jnp.bfloat16


def split_matrix(values):
    high = values.astype(np.float32).astype(ml_dtypes.bfloat16)
    low = (values - high.astype(np.float64)).astype(np.float32).astype(ml_dtypes.bfloat16)
    return np.stack([high, low])


def stencil_matrices(depth, plane):
    weight = {0: 0.0}
    for distance in range(1, 5):
        weight[distance] = weight[-distance] = STENCIL[distance - 1]
    left = np.zeros((XB, depth, XB + 8, depth))
    beside = np.zeros((XB, depth, XB, depth))
    for x in range(XB):
        for z in range(depth):
            left[x, z, x + 4, z] += 3.0 * CENTRE
            for step in range(-4, 5):
                if step == 0:
                    continue
                left[x, z, x + 4 + step, z] += weight[step]
                if 0 <= z + step < depth:
                    left[x, z, x + 4, z + step] += weight[step]
                elif z + step < 0:
                    beside[x, z, x, z + step + depth] += weight[step]
                else:
                    beside[x, z, x, z + step - depth] += weight[step]
    right = np.zeros((plane, plane))
    for step in range(-4, 5):
        if step:
            right += weight[step] * np.eye(plane, k=step)
    rows = XB * depth
    return (
        split_matrix(left.reshape(rows, (XB + 8) * depth)),
        split_matrix(beside.reshape(rows, rows)),
        split_matrix(right),
    )


def dot(a, b):
    return jnp.dot(a, b, preferred_element_type=F32)


def dot3(a, b):
    return dot(a[0], b[0]) + dot(a[1], b[0]) + dot(a[0], b[1])


def kernel(
    shots,
    slabs,
    *refs,
):
    operands, refs = refs[:OPERANDS], refs[OPERANDS:]
    out, held, rest = refs[0], refs[1 : 1 + OPERANDS], refs[1 + OPERANDS :]
    compute(shots, slabs, operands, held, out, *rest)


def compute(
    shots,
    slabs,
    operands,
    held,
    out,
    load_sem,
    field_h,
    field_l,
    halo,
    lap,
    inj,
    hot,
    flag_own,
    flag_up,
    flag_down,
    side,
    straight,
    picked,
    forward,
    moved,
    send_row,
    got_row,
    send_col,
    got_col,
    own_sum,
    slab_send,
    slab_recv,
    moved_send,
    moved_recv,
    flag_send,
    flag_recv,
    side_send,
    side_recv,
    straight_send,
    straight_recv,
    picked_send,
    picked_recv,
    row_send,
    row_recv,
    col_send,
    col_recv,
):
    loads = [
        pltpu.make_async_copy(src, dst, load_sem.at[i])
        for i, (src, dst) in enumerate(zip(operands, held))
    ]
    vel, fwd, adj, anchor, source, wavelet, count, receiver, residual = held[:9]
    left_m, beside_m, right_m = held[9:]
    for load in loads:
        load.start()
    tile_x, depth, tile_y = vel.shape[1:]
    along_x, plane = fwd.shape[1], fwd.shape[3]
    blocks = along_x // XB
    chunks = tile_x // XB
    rows = XB * depth
    me = lax.axis_index("shot")
    layer = lax.axis_index("slab")
    home_row = me // TILES_Y
    home_col = me % TILES_Y
    has = {
        "left": home_col > 0,
        "right": home_col < TILES_Y - 1,
        "up": home_row > 0,
        "down": home_row < shots // TILES_Y - 1,
        "above": layer > 0,
        "below": layer < slabs - 1,
    }
    where = {
        "left": {"shot": me - 1},
        "right": {"shot": me + 1},
        "up": {"shot": me - TILES_Y},
        "down": {"shot": me + TILES_Y},
        "above": {"slab": layer - 1},
        "below": {"slab": layer + 1},
    }
    opposite = {
        "left": "right",
        "right": "left",
        "up": "down",
        "down": "up",
        "above": "below",
        "below": "above",
    }

    def copy_to(side_name, src, dst, send_sem, recv_sem):
        return pltpu.make_async_remote_copy(
            src_ref=src,
            dst_ref=dst,
            send_sem=send_sem,
            recv_sem=recv_sem,
            device_id=where[side_name],
            device_id_type=MESH,
        )

    def start(side_name, *parts):
        @pl.when(has[side_name])
        def _():
            copy_to(side_name, *parts).start()

    def arrived(side_name, *parts):
        source_side = opposite[side_name]

        @pl.when(has[source_side])
        def _():
            copy_to(source_side, *parts).wait_recv()

    def sent(side_name, *parts):
        @pl.when(has[side_name])
        def _():
            copy_to(side_name, *parts).wait_send()

    for name in has:

        @pl.when(has[name])
        def _(name=name):
            pl.semaphore_signal(
                pltpu.get_barrier_semaphore(), inc=1, device_id=where[name], device_id_type=MESH
            )

    @pl.when(jnp.logical_not(has["above"]))
    def _():
        halo[:, :, HALO:, :] = jnp.zeros((4, along_x, HALO, plane), F32)

    @pl.when(jnp.logical_not(has["below"]))
    def _():
        halo[:, :, :HALO, :] = jnp.zeros((4, along_x, HALO, plane), F32)

    for index, name in enumerate(("up", "down")):

        @pl.when(jnp.logical_not(has[name]))
        def _(index=index):
            got_row[index] = jnp.zeros(got_row.shape[1:], F32)

    for index, name in enumerate(("left", "right")):

        @pl.when(jnp.logical_not(has[name]))
        def _(index=index):
            got_col[index] = jnp.zeros(got_col.shape[1:], F32)

    edge = jnp.zeros((2, 4, depth, plane), BF16)
    field_h[:, :4] = edge
    field_l[:, :4] = edge
    field_h[:, along_x + 4 :] = edge
    field_l[:, along_x + 4 :] = edge

    loads[0].wait()
    loads[3].wait()
    row_up = (home_row - anchor[0, 0]).astype(F32)
    col_left = (home_col - anchor[0, 1]).astype(F32)
    flag_own[...] = jnp.full(flag_own.shape, col_left, F32)

    total = sum(has[name].astype(jnp.int32) for name in has)
    pl.semaphore_wait(pltpu.get_barrier_semaphore(), total)

    def slab_copy(name, index, src):
        layers = slice(0, HALO) if name == "above" else slice(depth - HALO, depth)
        way = 0 if name == "above" else 1
        return (
            name,
            src.at[:, layers, :],
            halo.at[index, :, layers, :],
            slab_send.at[index, way],
            slab_recv.at[index, way],
        )

    def flag_copy(name):
        dst = flag_down if name == "up" else flag_up
        way = 0 if name == "up" else 1
        return (name, flag_own, dst, flag_send.at[way], flag_recv.at[way])

    def chunk_of(k):
        return pl.ds(k * XB, XB)

    def side_copy(name, k):
        way = 0 if name == "right" else 1
        return (
            name,
            vel.at[0, chunk_of(k)],
            side.at[way, chunk_of(k)],
            side_send.at[way, k],
            side_recv.at[way, k],
        )

    def straight_copy(name):
        way = 0 if name == "down" else 1
        return (name, vel.at[0], straight.at[way], straight_send.at[way], straight_recv.at[way])

    def picked_copy(name, k):
        way = 0 if name == "down" else 1
        return (
            name,
            forward.at[way, chunk_of(k)],
            picked.at[way, chunk_of(k)],
            picked_send.at[way, k],
            picked_recv.at[way, k],
        )

    def row_copy(name, part, k):
        way = 0 if name == "down" else 1
        return (
            name,
            send_row.at[way, part, chunk_of(k)],
            got_row.at[way, part, chunk_of(k)],
            row_send.at[way, part, k],
            row_recv.at[way, part, k],
        )

    def col_copy(name, k):
        way = 0 if name == "right" else 1
        return (
            name,
            send_col.at[way, chunk_of(k)],
            got_col.at[way, chunk_of(k)],
            col_send.at[way, k],
            col_recv.at[way, k],
        )

    for name in ("up", "down"):
        start(*flag_copy(name))
    for k in range(chunks):
        for name in ("left", "right"):
            start(*side_copy(name, k))
        if k == 0:
            for load in loads[1:3]:
                load.wait()
            for index, src in enumerate((fwd.at[0], adj.at[0])):
                for name in ("above", "below"):
                    start(*slab_copy(name, index, src))
            for name in ("up", "down"):
                start(*straight_copy(name))

    def mask_of(flag_value, shape):
        return jnp.broadcast_to(flag_value, shape) > 0.5

    def split_to(high_ref, low_ref, index, at, value):
        high = value.astype(BF16)
        high_ref[index, at] = high
        low_ref[index, at] = (value - high.astype(F32)).astype(BF16)

    def split_field(index, src):
        @pl.loop(0, blocks)
        def _(b):
            split_to(field_h, field_l, index, pl.ds(b * XB + 4, XB), src[0, pl.ds(b * XB, XB)])

    def laplace(index, b, beside):
        wide = pl.ds(b * XB, XB + 8)
        shape = ((XB + 8) * depth, plane)
        block = (field_h[index, wide].reshape(shape), field_l[index, wide].reshape(shape))
        at = pl.ds(b * XB, XB)
        near = halo[beside, at].reshape(rows, plane)
        near_h = near.astype(BF16)
        near = (near_h, (near - near_h.astype(F32)).astype(BF16))
        inner = tuple(part[4 * depth : 4 * depth + rows] for part in block)
        summed = dot3((left_m[0], left_m[1]), block)
        summed = summed + dot3((beside_m[0], beside_m[1]), near)
        summed = summed + dot3(inner, (right_m[0], right_m[1]))
        return summed.reshape(XB, depth, plane)

    def first_laplace(index):
        @pl.loop(0, blocks)
        def _(b):
            lap[index, pl.ds(b * XB, XB)] = laplace(index, b, index)

    first_layer = layer * depth
    total_depth = depth * slabs

    def whole_part(value, divisor):
        return ((value.astype(F32) + 0.5) * (1.0 / divisor)).astype(jnp.int32)

    def injections(index, positions, amounts):
        lanes = positions.shape[1]
        line = whole_part(positions, plane)
        cell_y = positions - line * plane
        cell_x = whole_part(line, total_depth)
        cell_z = line - cell_x * total_depth - first_layer
        inside = (cell_z >= 0) & (cell_z < depth)
        row_index = jnp.where(inside, cell_x * depth + cell_z, -1)
        col_hot = lax.broadcasted_iota(jnp.int32, (plane, lanes), 0) == cell_y
        for step in range(2):
            amount = amounts[step]
            high = amount.astype(BF16).astype(F32)
            for part, value in enumerate((high, amount - high)):
                at = (2 * step + part) * plane
                hot[at : at + plane, :lanes] = jnp.where(col_hot, value, 0.0).astype(BF16)
        tall = 2 * rows

        @pl.loop(0, along_x * depth // tall)
        def _(b):
            ids = lax.broadcasted_iota(jnp.int32, (tall, lanes), 0) + b * tall
            rows_hot = jnp.where(ids == row_index, 1.0, 0.0).astype(BF16)
            for step in range(2):
                cols = hot[2 * step * plane : 2 * (step + 1) * plane, :lanes]
                both = lax.dot_general(
                    rows_hot, cols, (((1,), (1,)), ((), ())), preferred_element_type=F32
                )
                added = both[:, :plane] + both[:, plane:]
                inj[2 * index + step, pl.ds(b * 2 * XB, 2 * XB)] = added.reshape(
                    2 * XB, depth, plane
                )

    def pass_on(k):
        for name in ("left", "right"):
            arrived(*side_copy(name, k))
        if k == 0:
            for name in ("up", "down"):
                arrived(*flag_copy(name))
        for way, flag in ((1, flag_up), (0, flag_down)):
            picks = mask_of(flag[...][None], (XB, depth, tile_y))
            forward[way, chunk_of(k)] = jnp.where(picks, side[0, chunk_of(k)], side[1, chunk_of(k)])
        for name in ("up", "down"):
            start(*picked_copy(name, k))

    for load in loads[4:]:
        load.wait()
    split_field(0, fwd)
    split_field(1, adj)
    lane = lax.broadcasted_iota(jnp.int32, source.shape, 1)
    active = jnp.where(lane < count[0], 1.0, 0.0)
    injections(0, source[...], (wavelet[0, 0:1] * active, wavelet[0, 1:2] * active))
    pass_on(0)
    for index in range(2):
        for name in ("above", "below"):
            arrived(*slab_copy(name, index, (fwd, adj)[index].at[0]))
    first_laplace(0)
    pass_on(1)
    injections(1, receiver[...], (residual[0, 1:2], residual[0, 0:1]))
    pass_on(2)
    first_laplace(1)
    pass_on(3)
    for k in range(4, chunks):
        pass_on(k)
    for name in ("up", "down"):
        arrived(*straight_copy(name))

    shape = (XB, depth, tile_y)
    is_left = mask_of(jnp.full(shape, col_left, F32), shape)
    is_up = mask_of(jnp.full(shape, row_up, F32), shape)

    def coefficient(part_row, k):
        at = chunk_of(k)
        own_same, own_other = vel[0, at], jnp.where(is_left, side[0, at], side[1, at])
        same, other = straight[part_row, at], picked[part_row, at]
        own_here = is_up if part_row == 1 else jnp.logical_not(is_up)
        same = jnp.where(own_here, own_same, same)
        other = jnp.where(own_here, own_other, other)
        speeds = jnp.concatenate(
            [jnp.where(is_left, other, same), jnp.where(is_left, same, other)], axis=2
        )
        return speeds * speeds

    def moved_copy(name, index, b):
        layers = slice(0, HALO) if name == "above" else slice(depth - HALO, depth)
        way = 0 if name == "above" else 1
        at = pl.ds(b * XB, XB)
        return (
            name,
            moved.at[index, at, layers, :],
            halo.at[2 + index, at, layers, :],
            moved_send.at[index, way, b],
            moved_recv.at[index, way, b],
        )

    for k in range(chunks):
        for name in ("up", "down"):
            arrived(*picked_copy(name, k))
        for part_row in range(2):
            squares = coefficient(part_row, k)
            x = part_row * tile_x + k * XB
            at = pl.ds(x, XB)
            for index, src in enumerate((fwd, adj)):
                change = squares * lap[index, at] + inj[2 * index, at]
                lap[index, at] = change
                later = src[0, at] + change
                moved[index, at] = later
                split_to(field_h, field_l, index, pl.ds(x + 4, XB), later)
                for name in ("above", "below"):
                    start(*moved_copy(name, index, part_row * chunks + k))

    def image(part_row, k):
        squares = coefficient(part_row, k)
        x = part_row * tile_x + k * XB
        b = part_row * chunks + k
        at = pl.ds(x, XB)
        second = squares * laplace(0, b, 2) + inj[1, at]
        back = squares * laplace(1, b, 3) + inj[3, at]
        later = moved[1, at]
        earlier = 2.0 * later - adj[0, at] + back
        whole = earlier * lap[0, at] + later * second
        low, high = whole[:, :, :tile_y], whole[:, :, tile_y:]
        return jnp.where(is_left, high, low), jnp.where(is_left, low, high)

    def along_row(k):
        at = chunk_of(k)
        for name in ("up", "down"):
            arrived(*row_copy(name, 0, k))
        for way, flag in ((0, flag_up), (1, flag_down)):
            picks = mask_of(flag[...][None], shape)
            piece = got_row[way, 0, at]
            send_col[1, at] = send_col[1, at] + jnp.where(picks, piece, 0.0)
            send_col[0, at] = send_col[0, at] + jnp.where(picks, 0.0, piece)
        for name in ("left", "right"):
            start(*col_copy(name, k))

    for k in range(chunks):
        at = chunk_of(k)
        for part_row in range(2):
            for index in range(2):
                for name in ("above", "below"):
                    arrived(*moved_copy(name, index, part_row * chunks + k))
        first_same, first_other = image(0, k)
        last_same, last_other = image(1, k)
        send_row[1, 0, at] = jnp.where(is_up, first_other, 0.0)
        send_row[0, 0, at] = jnp.where(is_up, 0.0, last_other)
        for name in ("up", "down"):
            start(*row_copy(name, 0, k))
        send_row[1, 1, at] = jnp.where(is_up, first_same, 0.0)
        send_row[0, 1, at] = jnp.where(is_up, 0.0, last_same)
        for name in ("up", "down"):
            start(*row_copy(name, 1, k))
        own_sum[at] = jnp.where(is_up, last_same, first_same)
        own_other = jnp.where(is_up, last_other, first_other)
        send_col[1, at] = jnp.where(is_left, own_other, 0.0)
        send_col[0, at] = jnp.where(is_left, 0.0, own_other)
        if k:
            along_row(k - 1)
    along_row(chunks - 1)
    for k in range(chunks):
        at = chunk_of(k)
        for name in ("up", "down"):
            arrived(*row_copy(name, 1, k))
        for name in ("left", "right"):
            arrived(*col_copy(name, k))
        summed = own_sum[at] + got_row[0, 1, at] + got_row[1, 1, at]
        out[0, at] = summed + got_col[0, at] + got_col[1, at]

    for name in ("up", "down"):
        sent(*flag_copy(name))
        sent(*straight_copy(name))
        for k in range(chunks):
            sent(*picked_copy(name, k))
            for part in range(2):
                sent(*row_copy(name, part, k))
    for name in ("left", "right"):
        for k in range(chunks):
            sent(*side_copy(name, k))
            sent(*col_copy(name, k))
    for index in range(2):
        for name in ("above", "below"):
            sent(*slab_copy(name, index, (fwd, adj)[index].at[0]))
            for b in range(blocks):
                sent(*moved_copy(name, index, b))


def body(shots, slabs, velocity, fwd_field, adj_field, anchor, source, wavelet, count, receiver, residual):
    tile_x, depth, tile_y = velocity.shape[1:]
    along_x, plane = fwd_field.shape[1], fwd_field.shape[3]
    chunks = tile_x // XB
    left_m, beside_m, right_m = (jnp.asarray(m) for m in stencil_matrices(depth, plane))
    vmem = pl.BlockSpec(memory_space=pltpu.VMEM)
    operands = (
        velocity, fwd_field, adj_field, anchor, source, wavelet, count, receiver, residual,
        left_m, beside_m, right_m,
    )
    scalars = (3, 6)
    aperture = (along_x, depth, plane)
    tile = (tile_x, depth, tile_y)
    dma = pltpu.SemaphoreType.DMA
    lanes = receiver.shape[1]
    summed = pl.pallas_call(
        functools.partial(kernel, shots, slabs),
        out_shape=jax.ShapeDtypeStruct(velocity.shape, F32),
        in_specs=[pl.BlockSpec(memory_space=pltpu.HBM)] * OPERANDS,
        out_specs=vmem,
        scratch_shapes=[
            (pltpu.SMEM if i in scalars else pltpu.VMEM)(operand.shape, operand.dtype)
            for i, operand in enumerate(operands)
        ]
        + [
            dma((OPERANDS,)),
            pltpu.VMEM((2, along_x + 8, depth, plane), BF16),
            pltpu.VMEM((2, along_x + 8, depth, plane), BF16),
            pltpu.VMEM((4,) + aperture, F32),
            pltpu.VMEM((2,) + aperture, F32),
            pltpu.VMEM((4,) + aperture, F32),
            pltpu.VMEM((4 * plane, lanes), BF16),
            pltpu.VMEM((depth, tile_y), F32),
            pltpu.VMEM((depth, tile_y), F32),
            pltpu.VMEM((depth, tile_y), F32),
            pltpu.VMEM((2,) + tile, F32),
            pltpu.VMEM((2,) + tile, F32),
            pltpu.VMEM((2,) + tile, F32),
            pltpu.VMEM((2,) + tile, F32),
            pltpu.VMEM((2,) + aperture, F32),
            pltpu.VMEM((2, 2) + tile, F32),
            pltpu.VMEM((2, 2) + tile, F32),
            pltpu.VMEM((2,) + tile, F32),
            pltpu.VMEM((2,) + tile, F32),
            pltpu.VMEM(tile, F32),
            dma((2, 2)),
            dma((2, 2)),
            dma((2, 2, 2 * chunks)),
            dma((2, 2, 2 * chunks)),
            dma((2,)),
            dma((2,)),
            dma((2, chunks)),
            dma((2, chunks)),
            dma((2,)),
            dma((2,)),
            dma((2, chunks)),
            dma((2, chunks)),
            dma((2, 2, chunks)),
            dma((2, 2, chunks)),
            dma((2, chunks)),
            dma((2, chunks)),
        ],
        compiler_params=pltpu.CompilerParams(
            collective_id=0, has_side_effects=True, vmem_limit_bytes=60 * 1024 * 1024
        ),
    )(*operands)
    return 2.0 * velocity * summed


def solution(mesh):
    placed = (
        P("shot", None, "slab", None),
        P("shot", None, "slab", None),
        P("shot", None, "slab", None),
        P("shot", None),
        P("shot", None),
        P("shot", None, None),
        P("shot"),
        P("shot", None),
        P("shot", None, None),
    )
    return jax.shard_map(
        functools.partial(body, mesh.shape["shot"], mesh.shape["slab"]),
        mesh=mesh,
        in_specs=placed,
        out_specs=P("shot", None, "slab", None),
        check_vma=False,
    )
```
